32 devices in a mesh: space: 4 (over z), tm: 8 (over y, x, core).
Axes of the slice: x: 2, y: 2, z: 4, core: 2. Of those that a mesh axis runs over, the one named last changes fastest.
Arguments:
- snapshots: float32 [8192, 3072], P('space', 'tm'), may hold values from -40 to 40, as said below
Outputs:
- window_gram: float32 [3072, 3072], P('tm', 'space')
The draws below stay inside these ranges and needn't reach their ends.
Inputs may be any that keep to these rules, and one draw needn't show every extreme that they name: `snapshots`: real-valued snapshot entries.
All inputs are finite; a program needn't handle non-finite values.
Results may differ from the reference program's by a relative error of at most 0.000058.
Values sent between devices are 32-bit elements; how exact they have to be, the bound alone decides.
No kernel may reach another device: no remote copies, remote signals or barrier semaphores. Data moves between devices by JAX's collectives and lax.ppermute only.
A program may use at most 128 MiB of HBM per device.

```python
import math
import jax
import jax.numpy as jnp
from jax import lax

WINDOW = 16
ROWS = 8192
FRAME_COUNT_ALL = 3072


def draw_snapshots(key, part):
    key = jax.random.fold_in(key, 11)
    subkeys = jax.random.split(key, 9)
    mode_count = min(512, ROWS // 2)
    along_each_line = 4
    picked_entries = jax.random.randint(subkeys[0], (ROWS, along_each_line), 0, mode_count)
    record_moments = jnp.arange(FRAME_COUNT_ALL, dtype=jnp.float32)[None, None, :]
    oscillation_rate = jnp.exp(jax.random.uniform(subkeys[1], (mode_count, 3, 1), jnp.float32, math.log(0.003), math.log(0.4)))
    cycle_offsets_radians = jax.random.uniform(subkeys[2], (mode_count, 3, 1), jnp.float32, -math.pi, math.pi)
    mean_flow_profile = 0.6 * jnp.sum(jnp.cos(oscillation_rate * record_moments + cycle_offsets_radians), axis=1)
    rough_part = 0.7 * jnp.clip(jax.random.normal(subkeys[3], (mode_count, FRAME_COUNT_ALL), jnp.float32), -5.0, 5.0)
    loadings = 0.5 * jnp.clip(jax.random.normal(subkeys[5], (ROWS, along_each_line), jnp.float32), -3.0, 3.0)
    jitter = 0.4 * jnp.clip(jax.random.normal(subkeys[6], (ROWS, FRAME_COUNT_ALL), jnp.float32), -5.0, 5.0)
    temporal = mean_flow_profile + rough_part
    velocity = jitter
    for column_slice in range(along_each_line):
        velocity = velocity + loadings[:, column_slice:column_slice + 1] * jnp.take(temporal, picked_entries[:, column_slice], axis=0)
    amplitude = jnp.exp(jax.random.uniform(subkeys[7], (ROWS, 1), jnp.float32, math.log(0.5), math.log(2.0)))
    scales = jnp.exp(jax.random.uniform(subkeys[8], (1, FRAME_COUNT_ALL), jnp.float32, math.log(0.3), math.log(3.0)))
    return jnp.clip(scales * amplitude * velocity, -40.0, 40.0)


def setup_inputs(seed: int = 0) -> dict:
    seeds = jax.random.split(jax.random.key(seed), 2)
    snapshots = draw_snapshots(jax.random.fold_in(seeds[1], 71), 0)
    return dict(snapshots=snapshots)


def reference(snapshots):
    gram = jnp.dot(snapshots.T, snapshots, precision=lax.Precision.HIGHEST, preferred_element_type=jnp.float32) / ROWS
    padded = jnp.pad(gram, ((0, WINDOW - 1), (0, WINDOW - 1)))
    total = jnp.zeros((FRAME_COUNT_ALL, FRAME_COUNT_ALL), jnp.float32)
    for offset in range(WINDOW):
        total = total + padded[offset:offset + FRAME_COUNT_ALL, offset:offset + FRAME_COUNT_ALL]
    return total / WINDOW
```

```python
import jax
import jax.numpy as jnp
from jax import lax
from jax.sharding import PartitionSpec as P

WINDOW = 16
CHUNKS = 3


def cross(left, right):
    return lax.dot_general(
        left,
        right,
        (((0,), (0,)), ((), ())),
        precision=lax.Precision.HIGH,
        preferred_element_type=jnp.float32,
    )


def swapped(block, bit):
    size = lax.axis_size("tm")
    return lax.ppermute(block, "tm", [(i, i ^ bit) for i in range(size)])


def shifted(block, axis, distance):
    devices = range(lax.axis_size(axis))
    route = [(i - distance, i) for i in devices if i - distance in devices]
    return lax.ppermute(block, axis, route)


def halves(block):
    if isinstance(block, tuple):
        return block
    half = block.shape[0] // 2
    return block[:half], block[half:]


def gathered(chunk, chips):
    blocks = {0: chunk}
    for offset in sorted(range(1, chips), key=lambda o: (bin(o).count("1"), o)):
        low, high = offset & -offset, 1 << (offset.bit_length() - 1)
        if low == high:
            blocks[offset] = swapped(chunk, 2 * offset)
        else:
            first = swapped(halves(blocks[offset ^ high])[0], 2 * high)
            second = swapped(halves(blocks[offset ^ low])[1], 2 * low)
            blocks[offset] = (first, second)
    return blocks


def product(rows, block):
    if isinstance(block, tuple):
        half = rows.shape[0] // 2
        return cross(rows[:half], block[0]) + cross(rows[half:], block[1])
    return cross(rows, block)


def local(snapshots):
    tm, space = lax.axis_index("tm"), lax.axis_index("space")
    chips, steps = lax.axis_size("tm") // 2, lax.axis_size("space")
    core, place = tm % 2, tm // 2
    block = snapshots.shape[1]
    width = block // CHUNKS
    scale = 1.0 / (snapshots.shape[0] * steps * WINDOW)
    reach = WINDOW - 1

    mate = swapped(snapshots, 1)
    gathers = []
    for j in range(CHUNKS):
        chunk = snapshots[:, j * width : (j + 1) * width]
        if j:
            chunk, mate, gathers[-1][1], gathers[-1][2] = lax.optimization_barrier(
                (chunk, mate, gathers[-1][1], gathers[-1][2])
            )
        gathers.append(gathered(chunk, chips))
    mine, theirs = [], []
    for blocks in gathers:
        partials = []
        for offset in range(chips):
            partials.append(
                jnp.concatenate(
                    [product(snapshots, blocks[offset]), product(mate, blocks[offset])], 0
                )
            )
        stacked = jnp.stack(partials)

        def term(share):
            return lax.dynamic_index_in_dim(
                stacked, lax.bitwise_xor(place, share), keepdims=False
            )

        right = left = jnp.zeros((2 * block, width), jnp.float32)
        for step in range(steps - 1):
            ahead = jnp.clip(steps - 1 - step + space, 0, steps - 1)
            behind = jnp.clip(step - (steps - 1 - space), 0, steps - 1)
            right = shifted(right + term(ahead), "space", 1)
            left = shifted(left + term(behind), "space", -1)
        total = (term(space) + right) + left
        mine.append(total[:block])
        theirs.append(total[block:])
    here = jnp.concatenate(mine, 1)
    there = swapped(jnp.concatenate(theirs, 1), 1)
    gram = jnp.where(
        core == 0,
        jnp.concatenate([here, there], 1),
        jnp.concatenate([there, here], 1),
    )
    share = 2 * block
    below = shifted(gram[:WINDOW], "tm", -1)
    beside = shifted(gram[:, :WINDOW].T, "space", -1)
    corner = shifted(shifted(gram[:WINDOW, :WINDOW], "tm", -1), "space", -1)
    extended = jnp.concatenate(
        [
            jnp.concatenate([gram, beside.T], 1),
            jnp.concatenate([below, corner], 1),
        ],
        0,
    )
    total = jnp.zeros((block, share), jnp.float32)
    for offset in range(WINDOW):
        total = total + extended[offset : offset + block, offset : offset + share]
    return total * scale


def solution(mesh):
    placed = (P("space", "tm"),)
    return jax.shard_map(
        local, mesh=mesh, in_specs=placed, out_specs=P("tm", "space"), check_vma=False
    )
```

```python
import functools

import jax
import jax.numpy as jnp
from jax import lax
from jax.experimental import pallas as pl
from jax.experimental.pallas import tpu as pltpu
from jax.sharding import PartitionSpec as P

WINDOW = 16
PARTS = (3, 3, 3, 2, 1)
DEPTH = 512
MEMORY = 48 * 2**20


def params():
    return pltpu.CompilerParams(vmem_limit_bytes=MEMORY)


def swapped(block, bit, axis="tm"):
    size = lax.axis_size(axis)
    return lax.ppermute(block, axis, [(i, i ^ bit) for i in range(size)])


def shifted(block, axis, distance):
    devices = range(lax.axis_size(axis))
    route = [(i - distance, i) for i in devices if i - distance in devices]
    return lax.ppermute(block, axis, route)


def split(value):
    high = value.astype(jnp.bfloat16)
    low = (value - high.astype(jnp.float32)).astype(jnp.bfloat16)
    return high, low


def turn_kernel(source, *chunks):
    turned = source[...].T
    start = 0
    for chunk in chunks:
        chunk[...] = turned[start : start + chunk.shape[0]]
        start += chunk.shape[0]


def turn(source, widths):
    rows, columns = source.shape
    step = 512
    return pl.pallas_call(
        turn_kernel,
        grid=(rows // step,),
        in_specs=[pl.BlockSpec((step, columns), lambda k: (k, 0))],
        out_specs=[pl.BlockSpec((width, step), lambda k: (0, k)) for width in widths],
        out_shape=[jax.ShapeDtypeStruct((width, rows), jnp.float32) for width in widths],
        compiler_params=params(),
    )(source)


def multiply_kernel(steps, place, own, mate, *refs):
    *pieces, keep, send, total = refs
    step = pl.program_id(0)
    left_high, left_low = split(jnp.concatenate([piece[...] for piece in pieces], 0))
    right_high, right_low = split(jnp.concatenate([own[...], mate[...]], 1))
    left = jnp.concatenate([left_high, left_low, left_high], 1)
    right = jnp.concatenate([right_high, right_high, right_low], 0)
    partial = jnp.dot(left, right, preferred_element_type=jnp.float32)

    @pl.when(step == 0)
    def _():
        total[...] = partial

    @pl.when(jnp.logical_and(step > 0, step < steps - 1))
    def _():
        total[...] += partial

    @pl.when(step == steps - 1)
    def _():
        ready = total[...] + partial
        count, width = keep.shape[:2]
        for offset in range(2 * count):
            block = ready[offset * width : (offset + 1) * width]
            distance = place[offset]
            slot, rest, bit = 0, lax.shift_right_logical(distance, 1), count // 2
            while bit:
                slot = slot + bit * lax.bitwise_and(rest, 1)
                rest, bit = lax.shift_right_logical(rest, 1), bit // 2
            odd = lax.bitwise_and(distance, 1)

            @pl.when(odd == 0)
            def _():
                keep[slot] = block

            @pl.when(odd == 1)
            def _():
                send[slot] = block


def multiply(place, own, mate, pieces):
    depth, block = own.shape
    steps = depth // DEPTH
    width = pieces[0].shape[0]
    chips = sum(piece.shape[0] for piece in pieces) // width
    shape = (chips // 2, width, 2 * block)
    right = pl.BlockSpec((DEPTH, block), lambda k: (k, 0))
    return pl.pallas_call(
        functools.partial(multiply_kernel, steps),
        grid=(steps,),
        in_specs=[pl.BlockSpec(memory_space=pltpu.SMEM), right, right]
        + [pl.BlockSpec((p.shape[0], DEPTH), lambda k: (0, k)) for p in pieces],
        out_specs=[pl.BlockSpec(shape, lambda k: (0, 0, 0))] * 2,
        out_shape=[jax.ShapeDtypeStruct(shape, jnp.float32)] * 2,
        scratch_shapes=[pltpu.VMEM((chips * width, 2 * block), jnp.float32)],
        compiler_params=params(),
        cost_estimate=pl.CostEstimate(flops=1, bytes_accessed=1, transcendentals=0),
    )(place, own, mate, *pieces)


def window_kernel(scale, turned, below, beside, corner, out, wide):
    rows, columns = out.shape
    wide[:rows, :columns] = turned[...].T
    wide[rows:, :columns] = below[...]
    edge = jnp.concatenate([beside[...].T, corner[:, :WINDOW]], 0)
    wide[:, columns:] = jnp.concatenate(
        [edge, jnp.zeros((rows + WINDOW, 128 - WINDOW), jnp.float32)], 1
    )
    total = wide[...] * scale
    distance = 1
    while distance < WINDOW:
        moved = pltpu.roll(total, total.shape[0] - distance, 0)
        total = total + pltpu.roll(moved, total.shape[1] - distance, 1)
        distance *= 2
    out[...] = total[:rows, :columns]


def window(scale, turned, below, beside, corner):
    columns, rows = turned.shape
    return pl.pallas_call(
        functools.partial(window_kernel, scale),
        out_shape=jax.ShapeDtypeStruct((rows, columns), jnp.float32),
        scratch_shapes=[pltpu.VMEM((rows + WINDOW, columns + 128), jnp.float32)],
        compiler_params=params(),
    )(turned, below, beside, corner)


def halve_kernel(keep, came, first, second):
    half = first.shape[0]
    first[...] = keep[:half] + came[:half]
    second[...] = keep[half:] + came[half:]


def halve(keep, came):
    half = (keep.shape[0] // 2,) + keep.shape[1:]
    return pl.pallas_call(
        halve_kernel,
        out_shape=[jax.ShapeDtypeStruct(half, jnp.float32)] * 2,
        compiler_params=params(),
    )(keep, came)


def collect_kernel(count, *refs):
    own, other = refs[2 * count :]
    start = 0
    for keep, came in zip(refs[:count], refs[count : 2 * count]):
        total = keep[0] + came[0]
        rows = pl.ds(start, total.shape[0])
        own[rows, :], other[rows, :] = total[:, : own.shape[1]], total[:, own.shape[1] :]
        start += total.shape[0]


def collect(keeps, cames):
    columns = sum(keep.shape[1] for keep in keeps)
    shape = jax.ShapeDtypeStruct((columns, keeps[0].shape[2] // 2), jnp.float32)
    return pl.pallas_call(
        functools.partial(collect_kernel, len(keeps)),
        out_shape=[shape] * 2,
        compiler_params=params(),
    )(*keeps, *cames)


def routed(block, ways):
    size = lax.axis_size("tm")
    return lax.ppermute(block, "tm", [(i, i ^ (2 << ways[i % 2])) for i in range(size)])


def local(snapshots):
    tm, space = lax.axis_index("tm"), lax.axis_index("space")
    chips, planes = lax.axis_size("tm") // 2, lax.axis_size("space")
    core = lax.rem(tm, 2)
    depth, block = snapshots.shape
    scale = 1.0 / (depth * planes * WINDOW)
    offsets = [jnp.int32(0), 1 + core, 2 - core, jnp.int32(3)]
    bit = 4
    while bit < chips:
        offsets += [lax.bitwise_xor(offset, bit) for offset in offsets]
        bit *= 2
    place = lax.bitwise_xor(jnp.stack(offsets), lax.bitwise_xor(lax.div(tm, 2), space))

    chunks = list(turn(snapshots, [block * part // sum(PARTS) for part in PARTS]))
    mate = swapped(snapshots, 1)
    count = len(chunks)
    steps = [(j, step) for j in range(count) for step in range(3)]
    got, firsts, halved, seconds = {}, {}, {}, {}

    def product(j):
        pieces = [chunks[j]] + [got[j, step] for step in range(3)]
        bit = 4
        while bit < chips:
            pieces += [swapped(piece, 2 * bit) for piece in pieces]
            bit *= 2
        keep, send = multiply(place, snapshots, mate, pieces)
        firsts[j] = keep, swapped(send, 1, "space")

    def halving(j):
        keep, send = halved[j]
        seconds[j] = keep, swapped(send, 2, "space")

    for k, (j, step) in enumerate(steps):
        tied = {"chunk": chunks[j]}
        if k >= 2:
            last = steps[k - 2]
            tied["got"] = got[last]
            if k == 2:
                tied["mate"] = mate
            i = last[0] if last[1] == 2 else -1
            if i >= 1:
                tied["halved"] = halve(*firsts[i - 1])
            if i >= 2:
                tied["second"] = seconds[i - 2]
            tied = lax.optimization_barrier(tied)
            chunks[j], got[last] = tied["chunk"], tied["got"]
            mate = tied.get("mate", mate)
            if i >= 1:
                halved[i - 1] = tied["halved"]
                halving(i - 1)
            if i >= 2:
                seconds[i - 2] = tied["second"]
        if step == 0:
            got[j, 0] = routed(chunks[j], (0, 1))
        elif step == 1:
            got[j, 1] = routed(chunks[j], (1, 0))
        else:
            got[j, 2] = routed(got[j, 0], (1, 0))
        if k >= 2 and i >= 0:
            product(i)
    for i in range(len(firsts), count):
        product(i)
    for i in range(count):
        if i not in halved:
            halved[i] = halve(*firsts[i])
            halving(i)
    for i, (keep, came) in seconds.items():
        bit = 2
        while keep.shape[0] > 1:
            bit *= 2
            keep, send = halve(keep, came)
            came = swapped(send, bit, "space")
        seconds[i] = keep, came
    own, other = collect(
        [seconds[j][0] for j in range(count)], [seconds[j][1] for j in range(count)]
    )
    other = swapped(other, 1)
    turned = jnp.concatenate(
        [jnp.where(core == 0, own, other), jnp.where(core == 0, other, own)], 0
    )
    below = shifted(turned[:, :WINDOW].T, "tm", -1)
    beside = shifted(turned[:WINDOW], "space", -1)
    corner = shifted(beside[:, :128].T[:WINDOW], "tm", -1)
    return window(scale, turned, below, beside, corner)


def solution(mesh):
    placed = (P("space", "tm"),)
    return jax.shard_map(
        local, mesh=mesh, in_specs=placed, out_specs=P("tm", "space"), check_vma=False
    )
```

```python
import functools

import jax
import jax.numpy as jnp
from jax import lax
from jax.experimental import pallas as pl
from jax.experimental.pallas import tpu as pltpu
from jax.sharding import PartitionSpec as P

WINDOW = 16
PARTS = (3, 3, 3, 2, 1)
DEPTH = 512
MEMORY = 10 * 2**20


def params(factor=1):
    return pltpu.CompilerParams(vmem_limit_bytes=factor * MEMORY)


def swapped(block, bit, axis="tm"):
    size = lax.axis_size(axis)
    return lax.ppermute(block, axis, [(i, i ^ bit) for i in range(size)])


def shifted(block, axis, distance):
    devices = range(lax.axis_size(axis))
    route = [(i - distance, i) for i in devices if i - distance in devices]
    return lax.ppermute(block, axis, route)


def split(value):
    high = value.astype(jnp.bfloat16)
    low = (value - high.astype(jnp.float32)).astype(jnp.bfloat16)
    return high, low


def turn_kernel(source, *chunks):
    turned = source[...].T
    start = 0
    for chunk in chunks:
        chunk[...] = turned[start : start + chunk.shape[0]]
        start += chunk.shape[0]


def turn(source, widths):
    rows, columns = source.shape
    step = 512
    return pl.pallas_call(
        turn_kernel,
        grid=(rows // step,),
        in_specs=[pl.BlockSpec((step, columns), lambda k: (k, 0))],
        out_specs=[pl.BlockSpec((width, step), lambda k: (0, k)) for width in widths],
        out_shape=[jax.ShapeDtypeStruct((width, rows), jnp.float32) for width in widths],
        compiler_params=params(),
    )(source)


def multiply_kernel(steps, place, own, mate, *refs):
    *pieces, keep, send, total = refs
    step = pl.program_id(0)
    left_high, left_low = split(jnp.concatenate([piece[...] for piece in pieces], 0))
    right_high, right_low = split(jnp.concatenate([own[...], mate[...]], 1))
    left = jnp.concatenate([left_high, left_low, left_high], 1)
    right = jnp.concatenate([right_high, right_high, right_low], 0)
    partial = jnp.dot(left, right, preferred_element_type=jnp.float32)

    @pl.when(step == 0)
    def _():
        total[...] = partial

    @pl.when(jnp.logical_and(step > 0, step < steps - 1))
    def _():
        total[...] += partial

    @pl.when(step == steps - 1)
    def _():
        ready = total[...] + partial
        count, width = keep.shape[:2]
        for offset in range(2 * count):
            block = ready[offset * width : (offset + 1) * width]
            distance = place[offset]
            slot, rest, bit = 0, lax.shift_right_logical(distance, 1), count // 2
            while bit:
                slot = slot + bit * lax.bitwise_and(rest, 1)
                rest, bit = lax.shift_right_logical(rest, 1), bit // 2
            odd = lax.bitwise_and(distance, 1)

            @pl.when(odd == 0)
            def _():
                keep[slot] = block

            @pl.when(odd == 1)
            def _():
                send[slot] = block


def multiply(place, own, mate, pieces):
    depth, block = own.shape
    steps = depth // DEPTH
    width = pieces[0].shape[0]
    chips = sum(piece.shape[0] for piece in pieces) // width
    shape = (chips // 2, width, 2 * block)
    right = pl.BlockSpec((DEPTH, block), lambda k: (k, 0))
    return pl.pallas_call(
        functools.partial(multiply_kernel, steps),
        grid=(steps,),
        in_specs=[pl.BlockSpec(memory_space=pltpu.SMEM), right, right]
        + [pl.BlockSpec((p.shape[0], DEPTH), lambda k: (0, k)) for p in pieces],
        out_specs=[pl.BlockSpec(shape, lambda k: (0, 0, 0))] * 2,
        out_shape=[jax.ShapeDtypeStruct(shape, jnp.float32)] * 2,
        scratch_shapes=[pltpu.VMEM((chips * width, 2 * block), jnp.float32)],
        compiler_params=params(chips // 2),
        cost_estimate=pl.CostEstimate(flops=1, bytes_accessed=1, transcendentals=0),
    )(place, own, mate, *pieces)


def window_kernel(scale, turned, below, beside, corner, out, wide):
    rows, columns = out.shape
    wide[:rows, :columns] = turned[...].T
    wide[rows:, :columns] = below[...]
    edge = jnp.concatenate([beside[...].T, corner[:, :WINDOW]], 0)
    wide[:, columns:] = jnp.concatenate(
        [edge, jnp.zeros((rows + WINDOW, 128 - WINDOW), jnp.float32)], 1
    )
    total = wide[...] * scale
    distance = 1
    while distance < WINDOW:
        moved = pltpu.roll(total, total.shape[0] - distance, 0)
        total = total + pltpu.roll(moved, total.shape[1] - distance, 1)
        distance *= 2
    out[...] = total[:rows, :columns]


def window(scale, turned, below, beside, corner):
    columns, rows = turned.shape
    return pl.pallas_call(
        functools.partial(window_kernel, scale),
        out_shape=jax.ShapeDtypeStruct((rows, columns), jnp.float32),
        scratch_shapes=[pltpu.VMEM((rows + WINDOW, columns + 128), jnp.float32)],
        compiler_params=params(),
    )(turned, below, beside, corner)


def halve_kernel(keep, came, first, second):
    half = first.shape[0]
    first[...] = keep[:half] + came[:half]
    second[...] = keep[half:] + came[half:]


def halve(keep, came):
    half = (keep.shape[0] // 2,) + keep.shape[1:]
    return pl.pallas_call(
        halve_kernel,
        out_shape=[jax.ShapeDtypeStruct(half, jnp.float32)] * 2,
        compiler_params=params(),
    )(keep, came)


def collect_kernel(count, *refs):
    own, other = refs[2 * count :]
    start = 0
    for keep, came in zip(refs[:count], refs[count : 2 * count]):
        total = keep[0] + came[0]
        rows = pl.ds(start, total.shape[0])
        own[rows, :], other[rows, :] = total[:, : own.shape[1]], total[:, own.shape[1] :]
        start += total.shape[0]


def collect(keeps, cames):
    columns = sum(keep.shape[1] for keep in keeps)
    shape = jax.ShapeDtypeStruct((columns, keeps[0].shape[2] // 2), jnp.float32)
    return pl.pallas_call(
        functools.partial(collect_kernel, len(keeps)),
        out_shape=[shape] * 2,
        compiler_params=params(),
    )(*keeps, *cames)


def routed(block, ways):
    size = lax.axis_size("tm")
    return lax.ppermute(block, "tm", [(i, i ^ (2 << ways[i % 2])) for i in range(size)])


def local(snapshots):
    tm, space = lax.axis_index("tm"), lax.axis_index("space")
    chips, planes = lax.axis_size("tm") // 2, lax.axis_size("space")
    core = lax.rem(tm, 2)
    depth, block = snapshots.shape
    scale = 1.0 / (depth * planes * WINDOW)
    offsets = [jnp.int32(0), 1 + core, 2 - core, jnp.int32(3)]
    bit = 4
    while bit < chips:
        offsets += [lax.bitwise_xor(offset, bit) for offset in offsets]
        bit *= 2
    place = lax.bitwise_xor(jnp.stack(offsets), lax.bitwise_xor(lax.div(tm, 2), space))

    chunks = list(turn(snapshots, [block * part // sum(PARTS) for part in PARTS]))
    mate = swapped(snapshots, 1)
    count = len(chunks)
    steps = [(j, step) for j in range(count) for step in range(3)]
    got, firsts, halved, seconds = {}, {}, {}, {}

    def product(j):
        pieces = [chunks[j]] + [got[j, step] for step in range(3)]
        bit = 4
        while bit < chips:
            pieces += [swapped(piece, 2 * bit) for piece in pieces]
            bit *= 2
        keep, send = multiply(place, snapshots, mate, pieces)
        firsts[j] = keep, swapped(send, 1, "space")

    def halving(j):
        keep, send = halved[j]
        seconds[j] = keep, swapped(send, 2, "space")

    for k, (j, step) in enumerate(steps):
        tied = {"chunk": chunks[j]}
        if k >= 2:
            last = steps[k - 2]
            tied["got"] = got[last]
            if k == 2:
                tied["mate"] = mate
            i = last[0] if last[1] == 2 else -1
            half = last[0] - 2 if last[1] == 0 and last[0] < count - 1 else -1
            late = last[0] - 3 if last[1] == 1 else -1
            if half in firsts:
                tied["halved"] = halve(*firsts[half])
            if late in seconds:
                tied["second"] = seconds[late]
            tied = lax.optimization_barrier(tied)
            chunks[j], got[last] = tied["chunk"], tied["got"]
            mate = tied.get("mate", mate)
            if half in firsts:
                halved[half] = tied["halved"]
                halving(half)
            if late in seconds:
                seconds[late] = tied["second"]
        if step == 0:
            got[j, 0] = routed(chunks[j], (0, 1))
        elif step == 1:
            got[j, 1] = routed(chunks[j], (1, 0))
        else:
            got[j, 2] = routed(got[j, 0], (1, 0))
        if k >= 2 and i >= 0:
            product(i)
    for i in range(len(firsts), count):
        tied = {"place": place}
        if i - 2 not in halved:
            tied["halved"] = halve(*firsts[i - 2])
        if i - 3 in seconds:
            tied["second"] = seconds[i - 3]
        tied = lax.optimization_barrier(tied)
        place = tied["place"]
        if i - 2 not in halved:
            halved[i - 2] = tied["halved"]
            halving(i - 2)
        if i - 3 in seconds:
            seconds[i - 3] = tied["second"]
        product(i)
    for i in range(count):
        if i not in halved:
            halved[i] = halve(*firsts[i])
            halving(i)
    for i, (keep, came) in seconds.items():
        bit = 2
        while keep.shape[0] > 1:
            bit *= 2
            keep, send = halve(keep, came)
            came = swapped(send, bit, "space")
        seconds[i] = keep, came
    own, other = collect(
        [seconds[j][0] for j in range(count)], [seconds[j][1] for j in range(count)]
    )
    other = swapped(other, 1)
    turned = jnp.concatenate(
        [jnp.where(core == 0, own, other), jnp.where(core == 0, other, own)], 0
    )
    below = shifted(turned[:, :WINDOW].T, "tm", -1)
    beside = shifted(turned[:WINDOW], "space", -1)
    corner = shifted(beside[:, :128].T[:WINDOW], "tm", -1)
    return window(scale, turned, below, beside, corner)


def solution(mesh):
    placed = (P("space", "tm"),)
    return jax.shard_map(
        local, mesh=mesh, in_specs=placed, out_specs=P("tm", "space"), check_vma=False
    )
```

```python
import functools

import jax
import jax.numpy as jnp
from jax import lax
from jax.experimental import pallas as pl
from jax.experimental.pallas import tpu as pltpu
from jax.sharding import PartitionSpec as P

WINDOW = 16
FLIGHT = 3
PARTS = (3, 3, 3, 2, 1)
DEPTH = 512
MEMORY = 12 * 2**20


def params(factor=1):
    return pltpu.CompilerParams(vmem_limit_bytes=factor * MEMORY)


def swapped(block, bit, axis="tm"):
    size = lax.axis_size(axis)
    return lax.ppermute(block, axis, [(i, i ^ bit) for i in range(size)])


def shifted(block, axis, distance):
    devices = range(lax.axis_size(axis))
    route = [(i - distance, i) for i in devices if i - distance in devices]
    return lax.ppermute(block, axis, route)


def split(value):
    high = value.astype(jnp.bfloat16)
    low = (value - high.astype(jnp.float32)).astype(jnp.bfloat16)
    return high, low


def turn_kernel(source, *chunks):
    turned = source[...].T
    start = 0
    for chunk in chunks:
        chunk[...] = turned[start : start + chunk.shape[0]]
        start += chunk.shape[0]


def turn(source, widths):
    rows, columns = source.shape
    step = 512
    return pl.pallas_call(
        turn_kernel,
        grid=(rows // step,),
        in_specs=[pl.BlockSpec((step, columns), lambda k: (k, 0))],
        out_specs=[pl.BlockSpec((width, step), lambda k: (0, k)) for width in widths],
        out_shape=[jax.ShapeDtypeStruct((width, rows), jnp.float32) for width in widths],
        compiler_params=params(),
    )(source)


def multiply_kernel(steps, place, own, mate, *refs):
    *pieces, keep, send, total = refs
    step = pl.program_id(0)
    left_high, left_low = split(jnp.concatenate([piece[...] for piece in pieces], 0))
    right_high, right_low = split(jnp.concatenate([own[...], mate[...]], 1))
    left = jnp.concatenate([left_high, left_low, left_high], 1)
    right = jnp.concatenate([right_high, right_high, right_low], 0)
    partial = jnp.dot(left, right, preferred_element_type=jnp.float32)

    @pl.when(step == 0)
    def _():
        total[...] = partial

    @pl.when(jnp.logical_and(step > 0, step < steps - 1))
    def _():
        total[...] += partial

    @pl.when(step == steps - 1)
    def _():
        ready = total[...] + partial
        count, width = keep.shape[:2]
        for offset in range(2 * count):
            block = ready[offset * width : (offset + 1) * width]
            distance = place[offset]
            slot, rest, bit = 0, lax.shift_right_logical(distance, 1), count // 2
            while bit:
                slot = slot + bit * lax.bitwise_and(rest, 1)
                rest, bit = lax.shift_right_logical(rest, 1), bit // 2
            odd = lax.bitwise_and(distance, 1)

            @pl.when(odd == 0)
            def _():
                keep[slot] = block

            @pl.when(odd == 1)
            def _():
                send[slot] = block


def multiply(place, own, mate, pieces):
    depth, block = own.shape
    steps = depth // DEPTH
    width = pieces[0].shape[0]
    chips = sum(piece.shape[0] for piece in pieces) // width
    shape = (chips // 2, width, 2 * block)
    right = pl.BlockSpec((DEPTH, block), lambda k: (k, 0))
    return pl.pallas_call(
        functools.partial(multiply_kernel, steps),
        grid=(steps,),
        in_specs=[pl.BlockSpec(memory_space=pltpu.SMEM), right, right]
        + [pl.BlockSpec((p.shape[0], DEPTH), lambda k: (0, k)) for p in pieces],
        out_specs=[pl.BlockSpec(shape, lambda k: (0, 0, 0))] * 2,
        out_shape=[jax.ShapeDtypeStruct(shape, jnp.float32)] * 2,
        scratch_shapes=[pltpu.VMEM((chips * width, 2 * block), jnp.float32)],
        compiler_params=params(5),
        cost_estimate=pl.CostEstimate(flops=1, bytes_accessed=1, transcendentals=0),
    )(place, own, mate, *pieces)


def window_kernel(scale, turned, below, beside, corner, out, wide):
    rows, columns = out.shape
    wide[:rows, :columns] = turned[...].T
    wide[rows:, :columns] = below[...]
    edge = jnp.concatenate([beside[...].T, corner[:, :WINDOW]], 0)
    wide[:, columns:] = jnp.concatenate(
        [edge, jnp.zeros((rows + WINDOW, 128 - WINDOW), jnp.float32)], 1
    )
    total = wide[...] * scale
    distance = 1
    while distance < WINDOW:
        moved = pltpu.roll(total, total.shape[0] - distance, 0)
        total = total + pltpu.roll(moved, total.shape[1] - distance, 1)
        distance *= 2
    out[...] = total[:rows, :columns]


def window(scale, turned, below, beside, corner):
    columns, rows = turned.shape
    return pl.pallas_call(
        functools.partial(window_kernel, scale),
        out_shape=jax.ShapeDtypeStruct((rows, columns), jnp.float32),
        scratch_shapes=[pltpu.VMEM((rows + WINDOW, columns + 128), jnp.float32)],
        compiler_params=params(),
    )(turned, below, beside, corner)


def halve_kernel(keep, came, first, second):
    half = first.shape[0]
    first[...] = keep[:half] + came[:half]
    second[...] = keep[half:] + came[half:]


def halve(keep, came):
    half = (keep.shape[0] // 2,) + keep.shape[1:]
    return pl.pallas_call(
        halve_kernel,
        out_shape=[jax.ShapeDtypeStruct(half, jnp.float32)] * 2,
        compiler_params=params(),
    )(keep, came)


def collect_kernel(count, *refs):
    own, other = refs[2 * count :]
    start = 0
    for keep, came in zip(refs[:count], refs[count : 2 * count]):
        total = keep[0] + came[0]
        rows = pl.ds(start, total.shape[0])
        own[rows, :], other[rows, :] = total[:, : own.shape[1]], total[:, own.shape[1] :]
        start += total.shape[0]


def collect(keeps, cames):
    columns = sum(keep.shape[1] for keep in keeps)
    shape = jax.ShapeDtypeStruct((columns, keeps[0].shape[2] // 2), jnp.float32)
    return pl.pallas_call(
        functools.partial(collect_kernel, len(keeps)),
        out_shape=[shape] * 2,
        compiler_params=params(),
    )(*keeps, *cames)


def routed(block, ways):
    size = lax.axis_size("tm")
    return lax.ppermute(block, "tm", [(i, i ^ (2 << ways[i % 2])) for i in range(size)])


def local(snapshots):
    tm, space = lax.axis_index("tm"), lax.axis_index("space")
    chips, planes = lax.axis_size("tm") // 2, lax.axis_size("space")
    core = lax.rem(tm, 2)
    depth, block = snapshots.shape
    scale = 1.0 / (depth * planes * WINDOW)
    offsets = [jnp.int32(0), 1 + core, 2 - core, jnp.int32(3)]
    bit = 4
    while bit < chips:
        offsets += [lax.bitwise_xor(offset, bit) for offset in offsets]
        bit *= 2
    place = lax.bitwise_xor(jnp.stack(offsets), lax.bitwise_xor(lax.div(tm, 2), space))

    chunks = list(turn(snapshots, [block * part // sum(PARTS) for part in PARTS]))
    mate = swapped(snapshots, 1)
    count = len(chunks)
    steps = [(0, 0)] + [(j + (step == 0), step) for j in range(count) for step in (1, 0, 2)]
    steps.remove((count, 0))
    got, firsts, halved, seconds = {}, {}, {}, {}

    def product(j):
        pieces = [chunks[j]] + [got[j, step] for step in range(3)]
        bit = 4
        while bit < chips:
            pieces += [swapped(piece, 2 * bit) for piece in pieces]
            bit *= 2
        keep, send = multiply(place, snapshots, mate, pieces)
        firsts[j] = keep, swapped(send, 1, "space")

    def halving(j):
        keep, send = halved[j]
        seconds[j] = keep, swapped(send, 2, "space")

    for k, (j, step) in enumerate(steps):
        tied = {"chunk": chunks[j]}
        ready = -1
        if k >= FLIGHT:
            last = steps[k - FLIGHT]
            tied["got"] = got[last]
            if k == FLIGHT:
                tied["mate"] = mate
            if k > FLIGHT:
                tied["before"] = chunks[steps[k - 1][0]]
            ready = last[0] if last[1] == 2 else -1
            half = len(firsts) - 2 if steps[k - FLIGHT - 1][1] == 2 and k > FLIGHT else -1
            late = -1
            if half in firsts:
                tied["halved"] = halve(*firsts[half])
            if late in seconds:
                tied["second"] = seconds[late]
            tied = lax.optimization_barrier(tied)
            if k > FLIGHT:
                chunks[steps[k - 1][0]] = tied["before"]
            chunks[j], got[last] = tied["chunk"], tied["got"]
            mate = tied.get("mate", mate)
            if half in firsts:
                halved[half] = tied["halved"]
                halving(half)
            if late in seconds:
                seconds[late] = tied["second"]
        if step == 0:
            got[j, 0] = routed(chunks[j], (0, 1))
        elif step == 1:
            got[j, 1] = routed(chunks[j], (1, 0))
        else:
            got[j, 2] = routed(got[j, 0], (1, 0))
        if ready >= 0:
            product(ready)
    for i in range(len(firsts), count):
        tied = {"place": place}
        if i - 2 not in halved:
            tied["halved"] = halve(*firsts[i - 2])
        if i - 3 in seconds:
            tied["second"] = seconds[i - 3]
        tied = lax.optimization_barrier(tied)
        place = tied["place"]
        if i - 2 not in halved:
            halved[i - 2] = tied["halved"]
            halving(i - 2)
        if i - 3 in seconds:
            seconds[i - 3] = tied["second"]
        product(i)
    for i in range(count):
        if i not in halved:
            halved[i] = halve(*firsts[i])
            halving(i)
    for i, (keep, came) in seconds.items():
        bit = 2
        while keep.shape[0] > 1:
            bit *= 2
            keep, send = halve(keep, came)
            came = swapped(send, bit, "space")
        seconds[i] = keep, came
    own, other = collect(
        [seconds[j][0] for j in range(count)], [seconds[j][1] for j in range(count)]
    )
    other = swapped(other, 1)
    turned = jnp.concatenate(
        [jnp.where(core == 0, own, other), jnp.where(core == 0, other, own)], 0
    )
    below = shifted(turned[:, :WINDOW].T, "tm", -1)
    beside = shifted(turned[:WINDOW], "space", -1)
    corner = shifted(beside[:, :128].T[:WINDOW], "tm", -1)
    return window(scale, turned, below, beside, corner)


def solution(mesh):
    placed = (P("space", "tm"),)
    return jax.shard_map(
        local, mesh=mesh, in_specs=placed, out_specs=P("tm", "space"), check_vma=False
    )
```

```python
import functools

import jax
import jax.numpy as jnp
from jax import lax
from jax.experimental import pallas as pl
from jax.experimental.pallas import tpu as pltpu
from jax.sharding import PartitionSpec as P

WINDOW = 16
FLIGHT = 3
PARTS = (3, 3, 3, 2, 1)
DEPTH = 512
MEMORY = 12 * 2**20


def params(factor=1):
    return pltpu.CompilerParams(vmem_limit_bytes=factor * MEMORY)


def swapped(block, bit, axis="tm"):
    size = lax.axis_size(axis)
    return lax.ppermute(block, axis, [(i, i ^ bit) for i in range(size)])


def shifted(block, axis, distance):
    devices = range(lax.axis_size(axis))
    route = [(i - distance, i) for i in devices if i - distance in devices]
    return lax.ppermute(block, axis, route)


def split(value):
    high = value.astype(jnp.bfloat16)
    low = (value - high.astype(jnp.float32)).astype(jnp.bfloat16)
    return high, low


def turn_kernel(source, *chunks):
    turned = source[...].T
    start = 0
    for chunk in chunks:
        chunk[...] = turned[start : start + chunk.shape[0]]
        start += chunk.shape[0]


def turn(source, widths):
    rows, columns = source.shape
    step = 512
    return pl.pallas_call(
        turn_kernel,
        grid=(rows // step,),
        in_specs=[pl.BlockSpec((step, columns), lambda k: (k, 0))],
        out_specs=[pl.BlockSpec((width, step), lambda k: (0, k)) for width in widths],
        out_shape=[jax.ShapeDtypeStruct((width, rows), jnp.float32) for width in widths],
        compiler_params=params(),
    )(source)


def multiply_kernel(steps, count, place, own, mate, *refs):
    pieces, (*earlier, keep, send, total) = refs[:count], refs[count:]
    step = pl.program_id(0)
    left_high, left_low = split(jnp.concatenate([piece[...] for piece in pieces], 0))
    right_high, right_low = split(jnp.concatenate([own[...], mate[...]], 1))
    left = jnp.concatenate([left_high, left_low, left_high], 1)
    right = jnp.concatenate([right_high, right_high, right_low], 0)
    partial = jnp.dot(left, right, preferred_element_type=jnp.float32)

    if earlier:
        kept, came, first, second = earlier

        @pl.when(step == 0)
        def _():
            half = first.shape[0]
            first[...] = kept[:half] + came[:half]
            second[...] = kept[half:] + came[half:]

    @pl.when(step == 0)
    def _():
        total[...] = partial

    @pl.when(jnp.logical_and(step > 0, step < steps - 1))
    def _():
        total[...] += partial

    @pl.when(step == steps - 1)
    def _():
        ready = total[...] + partial
        count, width = keep.shape[:2]
        for offset in range(2 * count):
            block = ready[offset * width : (offset + 1) * width]
            distance = place[offset]
            slot, rest, bit = 0, lax.shift_right_logical(distance, 1), count // 2
            while bit:
                slot = slot + bit * lax.bitwise_and(rest, 1)
                rest, bit = lax.shift_right_logical(rest, 1), bit // 2
            odd = lax.bitwise_and(distance, 1)

            @pl.when(odd == 0)
            def _():
                keep[slot] = block

            @pl.when(odd == 1)
            def _():
                send[slot] = block


def multiply(place, own, mate, pieces, earlier):
    depth, block = own.shape
    steps = depth // DEPTH
    width = pieces[0].shape[0]
    chips = sum(piece.shape[0] for piece in pieces) // width
    shape = (chips // 2, width, 2 * block)
    shapes = [(array.shape[0] // 2,) + array.shape[1:] for array in earlier] + [shape] * 2
    whole = lambda shape: pl.BlockSpec(shape, lambda k: (0, 0, 0))
    right = pl.BlockSpec((DEPTH, block), lambda k: (k, 0))
    return pl.pallas_call(
        functools.partial(multiply_kernel, steps, len(pieces)),
        grid=(steps,),
        in_specs=[pl.BlockSpec(memory_space=pltpu.SMEM), right, right]
        + [pl.BlockSpec((p.shape[0], DEPTH), lambda k: (0, k)) for p in pieces]
        + [whole(array.shape) for array in earlier],
        out_specs=[whole(shape) for shape in shapes],
        out_shape=[jax.ShapeDtypeStruct(shape, jnp.float32) for shape in shapes],
        scratch_shapes=[pltpu.VMEM((chips * width, 2 * block), jnp.float32)],
        compiler_params=params(5),
        cost_estimate=pl.CostEstimate(flops=1, bytes_accessed=1, transcendentals=0),
    )(place, own, mate, *pieces, *earlier)


def window_kernel(scale, turned, below, beside, corner, out, wide):
    rows, columns = out.shape
    wide[:rows, :columns] = turned[...].T
    wide[rows:, :columns] = below[...]
    edge = jnp.concatenate([beside[...].T, corner[:, :WINDOW]], 0)
    wide[:, columns:] = jnp.concatenate(
        [edge, jnp.zeros((rows + WINDOW, 128 - WINDOW), jnp.float32)], 1
    )
    total = wide[...] * scale
    distance = 1
    while distance < WINDOW:
        moved = pltpu.roll(total, total.shape[0] - distance, 0)
        total = total + pltpu.roll(moved, total.shape[1] - distance, 1)
        distance *= 2
    out[...] = total[:rows, :columns]


def window(scale, turned, below, beside, corner):
    columns, rows = turned.shape
    return pl.pallas_call(
        functools.partial(window_kernel, scale),
        out_shape=jax.ShapeDtypeStruct((rows, columns), jnp.float32),
        scratch_shapes=[pltpu.VMEM((rows + WINDOW, columns + 128), jnp.float32)],
        compiler_params=params(),
    )(turned, below, beside, corner)


def halve_kernel(keep, came, first, second):
    half = first.shape[0]
    first[...] = keep[:half] + came[:half]
    second[...] = keep[half:] + came[half:]


def halve(keep, came):
    half = (keep.shape[0] // 2,) + keep.shape[1:]
    return pl.pallas_call(
        halve_kernel,
        out_shape=[jax.ShapeDtypeStruct(half, jnp.float32)] * 2,
        compiler_params=params(),
    )(keep, came)


def collect_kernel(count, *refs):
    own, other = refs[2 * count :]
    start = 0
    for keep, came in zip(refs[:count], refs[count : 2 * count]):
        total = keep[0] + came[0]
        rows = pl.ds(start, total.shape[0])
        own[rows, :], other[rows, :] = total[:, : own.shape[1]], total[:, own.shape[1] :]
        start += total.shape[0]


def collect(keeps, cames):
    columns = sum(keep.shape[1] for keep in keeps)
    shape = jax.ShapeDtypeStruct((columns, keeps[0].shape[2] // 2), jnp.float32)
    return pl.pallas_call(
        functools.partial(collect_kernel, len(keeps)),
        out_shape=[shape] * 2,
        compiler_params=params(),
    )(*keeps, *cames)


def routed(block, ways):
    size = lax.axis_size("tm")
    return lax.ppermute(block, "tm", [(i, i ^ (2 << ways[i % 2])) for i in range(size)])


def local(snapshots):
    tm, space = lax.axis_index("tm"), lax.axis_index("space")
    chips, planes = lax.axis_size("tm") // 2, lax.axis_size("space")
    core = lax.rem(tm, 2)
    depth, block = snapshots.shape
    scale = 1.0 / (depth * planes * WINDOW)
    offsets = [jnp.int32(0), 1 + core, 2 - core, jnp.int32(3)]
    bit = 4
    while bit < chips:
        offsets += [lax.bitwise_xor(offset, bit) for offset in offsets]
        bit *= 2
    place = lax.bitwise_xor(jnp.stack(offsets), lax.bitwise_xor(lax.div(tm, 2), space))

    chunks = list(turn(snapshots, [block * part // sum(PARTS) for part in PARTS]))
    mate = swapped(snapshots, 1)
    count = len(chunks)
    steps = [(0, 0)] + [(j + (step == 0), step) for j in range(count) for step in (1, 0, 2)]
    steps.remove((count, 0))
    got, firsts, seconds = {}, {}, {}

    def product(j, earlier=()):
        pieces = [chunks[j]] + [got[j, step] for step in range(3)]
        bit = 4
        while bit < chips:
            pieces += [swapped(piece, 2 * bit) for piece in pieces]
            bit *= 2
        *halved, keep, send = multiply(place, snapshots, mate, pieces, earlier)
        firsts[j] = keep, swapped(send, 1, "space")
        if halved:
            seconds[j - 1] = halved[0], swapped(halved[1], 2, "space")

    for k, (j, step) in enumerate(steps):
        tied = {"chunk": chunks[j]}
        ready = -1
        if k >= FLIGHT:
            last = steps[k - FLIGHT]
            tied["got"] = got[last]
            if k == FLIGHT:
                tied["mate"] = mate
            if k > FLIGHT:
                tied["before"] = chunks[steps[k - 1][0]]
            ready = k // FLIGHT - 2 if k % FLIGHT == FLIGHT - 1 else -1
            tied = lax.optimization_barrier(tied)
            if k > FLIGHT:
                chunks[steps[k - 1][0]] = tied["before"]
            chunks[j], got[last] = tied["chunk"], tied["got"]
            mate = tied.get("mate", mate)
        if step == 0:
            got[j, 0] = routed(chunks[j], (0, 1))
        elif step == 1:
            got[j, 1] = routed(chunks[j], (1, 0))
        else:
            got[j, 2] = routed(got[j, 0], (1, 0))
        if ready >= 0:
            product(ready, firsts.get(ready - 1, ()))
    for i in range(len(firsts), count):
        if i == count - 1:
            place, seconds = lax.optimization_barrier((place, seconds))
        product(i, firsts[i - 1] if i == 2 else ())
    for i in range(count):
        if i not in seconds:
            keep, send = halve(*firsts[i])
            seconds[i] = keep, swapped(send, 2, "space")
    for i, (keep, came) in seconds.items():
        bit = 2
        while keep.shape[0] > 1:
            bit *= 2
            keep, send = halve(keep, came)
            came = swapped(send, bit, "space")
        seconds[i] = keep, came
    own, other = collect(
        [seconds[j][0] for j in range(count)], [seconds[j][1] for j in range(count)]
    )
    other = swapped(other, 1)
    turned = jnp.concatenate(
        [jnp.where(core == 0, own, other), jnp.where(core == 0, other, own)], 0
    )
    below = shifted(turned[:, :WINDOW].T, "tm", -1)
    beside = shifted(turned[:WINDOW], "space", -1)
    corner = shifted(beside[:, :128].T[:WINDOW], "tm", -1)
    return window(scale, turned, below, beside, corner)


def solution(mesh):
    placed = (P("space", "tm"),)
    return jax.shard_map(
        local, mesh=mesh, in_specs=placed, out_specs=P("tm", "space"), check_vma=False
    )
```

```python
import functools

import jax
import jax.numpy as jnp
from jax import lax
from jax.experimental import pallas as pl
from jax.experimental.pallas import tpu as pltpu
from jax.sharding import PartitionSpec as P

WINDOW = 16
FLIGHT = 3
PARTS = (3, 3, 3, 2, 1)
DEPTH = 512
MEMORY = 12 * 2**20


def params(factor=1):
    return pltpu.CompilerParams(vmem_limit_bytes=factor * MEMORY)


def swapped(block, bit, axis="tm"):
    size = lax.axis_size(axis)
    return lax.ppermute(block, axis, [(i, i ^ bit) for i in range(size)])


def shifted(block, axis, distance):
    devices = range(lax.axis_size(axis))
    route = [(i - distance, i) for i in devices if i - distance in devices]
    return lax.ppermute(block, axis, route)


def split(value):
    high = value.astype(jnp.bfloat16)
    low = (value - high.astype(jnp.float32)).astype(jnp.bfloat16)
    return high, low


def turn_kernel(source, *chunks):
    turned = source[...].T
    start = 0
    for chunk in chunks:
        chunk[...] = turned[start : start + chunk.shape[0]]
        start += chunk.shape[0]


def turn(source, widths):
    rows, columns = source.shape
    step = 512
    return pl.pallas_call(
        turn_kernel,
        grid=(rows // step,),
        in_specs=[pl.BlockSpec((step, columns), lambda k: (k, 0))],
        out_specs=[pl.BlockSpec((width, step), lambda k: (0, k)) for width in widths],
        out_shape=[jax.ShapeDtypeStruct((width, rows), jnp.float32) for width in widths],
        compiler_params=params(),
    )(source)


def multiply_kernel(steps, count, place, own, mate, *refs):
    pieces, (*earlier, keep, send, total) = refs[:count], refs[count:]
    step = pl.program_id(0)
    left_high, left_low = split(jnp.concatenate([piece[...] for piece in pieces], 0))
    right_high, right_low = split(jnp.concatenate([own[...], mate[...]], 1))
    left = jnp.concatenate([left_high, left_low, left_high], 1)
    right = jnp.concatenate([right_high, right_high, right_low], 0)
    partial = jnp.dot(left, right, preferred_element_type=jnp.float32)

    if earlier:
        kept, came, first, second = earlier

        @pl.when(step == 0)
        def _():
            half = first.shape[0]
            first[...] = kept[:half] + came[:half]
            second[...] = kept[half:] + came[half:]

    @pl.when(step == 0)
    def _():
        total[...] = partial

    @pl.when(jnp.logical_and(step > 0, step < steps - 1))
    def _():
        total[...] += partial

    @pl.when(step == steps - 1)
    def _():
        ready = total[...] + partial
        count, width = keep.shape[:2]
        for offset in range(2 * count):
            block = ready[offset * width : (offset + 1) * width]
            distance = place[offset]
            slot, rest, bit = 0, lax.shift_right_logical(distance, 1), count // 2
            while bit:
                slot = slot + bit * lax.bitwise_and(rest, 1)
                rest, bit = lax.shift_right_logical(rest, 1), bit // 2
            odd = lax.bitwise_and(distance, 1)

            @pl.when(odd == 0)
            def _():
                keep[slot] = block

            @pl.when(odd == 1)
            def _():
                send[slot] = block


def multiply(place, own, mate, pieces, earlier):
    depth, block = own.shape
    steps = depth // DEPTH
    width = pieces[0].shape[0]
    chips = sum(piece.shape[0] for piece in pieces) // width
    shape = (chips // 2, width, 2 * block)
    shapes = [(array.shape[0] // 2,) + array.shape[1:] for array in earlier] + [shape] * 2
    whole = lambda shape: pl.BlockSpec(shape, lambda k: (0, 0, 0))
    right = pl.BlockSpec((DEPTH, block), lambda k: (k, 0))
    return pl.pallas_call(
        functools.partial(multiply_kernel, steps, len(pieces)),
        grid=(steps,),
        in_specs=[pl.BlockSpec(memory_space=pltpu.SMEM), right, right]
        + [pl.BlockSpec((p.shape[0], DEPTH), lambda k: (0, k)) for p in pieces]
        + [whole(array.shape) for array in earlier],
        out_specs=[whole(shape) for shape in shapes],
        out_shape=[jax.ShapeDtypeStruct(shape, jnp.float32) for shape in shapes],
        scratch_shapes=[pltpu.VMEM((chips * width, 2 * block), jnp.float32)],
        compiler_params=params(5),
        cost_estimate=pl.CostEstimate(flops=1, bytes_accessed=1, transcendentals=0),
    )(place, own, mate, *pieces, *earlier)


def window_kernel(scale, core, own, swap, near, first, second, rim, out, wide):
    rows, columns = out.shape
    block = columns // 2

    @pl.when(core[0] == 0)
    def _():
        wide[:rows, :block] = own[...].T
        wide[:rows, block:columns] = swap[:, :block].T
        wide[rows:, :block] = near[...]
        wide[rows:, block:columns] = swap[:, block:].T[:WINDOW]

    @pl.when(core[0] == 1)
    def _():
        wide[:rows, :block] = swap[:, :block].T
        wide[:rows, block:columns] = own[...].T
        wide[rows:, :block] = first[...]
        wide[rows:, block:columns] = second[...]

    wide[:, columns:] = jnp.concatenate(
        [
            rim[...].T[: rows + WINDOW],
            jnp.zeros((rows + WINDOW, 128 - WINDOW), jnp.float32),
        ],
        1,
    )
    total = wide[...] * scale
    distance = 1
    while distance < WINDOW:
        moved = pltpu.roll(total, total.shape[0] - distance, 0)
        total = total + pltpu.roll(moved, total.shape[1] - distance, 1)
        distance *= 2
    out[...] = total[:rows, :columns]


def window(scale, core, own, *parts):
    columns, rows = own.shape
    return pl.pallas_call(
        functools.partial(window_kernel, scale),
        in_specs=[pl.BlockSpec(memory_space=pltpu.SMEM)]
        + [pl.BlockSpec(memory_space=pltpu.VMEM)] * (1 + len(parts)),
        out_shape=jax.ShapeDtypeStruct((rows, 2 * columns), jnp.float32),
        scratch_shapes=[pltpu.VMEM((rows + WINDOW, 2 * columns + 128), jnp.float32)],
        compiler_params=params(),
    )(core, own, *parts)


def halve_kernel(keep, came, first, second):
    half = first.shape[0]
    first[...] = keep[:half] + came[:half]
    second[...] = keep[half:] + came[half:]


def halve(keep, came):
    half = (keep.shape[0] // 2,) + keep.shape[1:]
    return pl.pallas_call(
        halve_kernel,
        out_shape=[jax.ShapeDtypeStruct(half, jnp.float32)] * 2,
        compiler_params=params(),
    )(keep, came)


def collect_kernel(count, *refs):
    own, swap, near, far = refs[2 * count :]
    block = own.shape[1]
    start = 0
    for keep, came in zip(refs[:count], refs[count : 2 * count]):
        total = keep[0] + came[0]
        rows = pl.ds(start, total.shape[0])
        own[rows, :] = total[:, :block]
        swap[rows, :block] = total[:, block:]
        start += total.shape[0]
    swap[:, block:] = own[:, :128]
    near[...] = swap[:, :128].T[:WINDOW]
    far[...] = own[:, :128].T[:WINDOW]


def collect(keeps, cames):
    columns = sum(keep.shape[1] for keep in keeps)
    block = keeps[0].shape[2] // 2
    shapes = [(columns, block), (columns, block + 128)] + [(WINDOW, columns)] * 2
    return pl.pallas_call(
        functools.partial(collect_kernel, len(keeps)),
        out_shape=[jax.ShapeDtypeStruct(shape, jnp.float32) for shape in shapes],
        compiler_params=params(),
    )(*keeps, *cames)


def moved(value, planes, size, source, target):
    pairs = []
    for chip in range(size // 2):
        start, end = source(chip), target(chip)
        if start < size:
            pairs += [((z + 1) * size + start, z * size + end) for z in range(planes - 1)]
    return lax.ppermute(value, ("space", "tm"), pairs)


def rimmed(edge, core, planes, size):
    block = edge.shape[1] // 2
    zero = moved(edge, planes, size, lambda chip: 2 * chip, lambda chip: 2 * chip)
    one = moved(edge, planes, size, lambda chip: 2 * chip, lambda chip: 2 * chip + 1)
    next_ = moved(
        edge[:, :128], planes, size, lambda chip: 2 * chip + 2, lambda chip: 2 * chip + 1
    )
    return jnp.where(
        core == 0, zero[:, : block + 128], jnp.concatenate([one[:, block:], next_], 1)
    )


def finished(keep, came):
    bit = 2
    while keep.shape[0] > 1:
        bit *= 2
        keep, send = halve(keep, came)
        came = swapped(send, bit, "space")
    return keep, came


def routed(block, ways):
    size = lax.axis_size("tm")
    return lax.ppermute(block, "tm", [(i, i ^ (2 << ways[i % 2])) for i in range(size)])


def local(snapshots):
    tm, space = lax.axis_index("tm"), lax.axis_index("space")
    chips, planes = lax.axis_size("tm") // 2, lax.axis_size("space")
    core = lax.rem(tm, 2)
    depth, block = snapshots.shape
    scale = 1.0 / (depth * planes * WINDOW)
    offsets = [jnp.int32(0), 1 + core, 2 - core, jnp.int32(3)]
    bit = 4
    while bit < chips:
        offsets += [lax.bitwise_xor(offset, bit) for offset in offsets]
        bit *= 2
    place = lax.bitwise_xor(jnp.stack(offsets), lax.bitwise_xor(lax.div(tm, 2), space))

    chunks = list(turn(snapshots, [block * part // sum(PARTS) for part in PARTS]))
    mate = swapped(snapshots, 1)
    count = len(chunks)
    steps = [(0, 0)] + [(j + (step == 0), step) for j in range(count) for step in (1, 0, 2)]
    steps.remove((count, 0))
    got, firsts, seconds = {}, {}, {}

    def product(j, earlier=()):
        pieces = [chunks[j]] + [got[j, step] for step in range(3)]
        bit = 4
        while bit < chips:
            pieces += [swapped(piece, 2 * bit) for piece in pieces]
            bit *= 2
        *halved, keep, send = multiply(place, snapshots, mate, pieces, earlier)
        firsts[j] = keep, swapped(send, 1, "space")
        if halved:
            seconds[j - 1] = halved[0], swapped(halved[1], 2, "space")

    for k, (j, step) in enumerate(steps):
        tied = {"chunk": chunks[j]}
        ready = -1
        if k >= FLIGHT:
            last = steps[k - FLIGHT]
            tied["got"] = got[last]
            if k == FLIGHT:
                tied["mate"] = mate
            if k > FLIGHT:
                tied["before"] = chunks[steps[k - 1][0]]
            ready = k // FLIGHT - 2 if k % FLIGHT == FLIGHT - 1 else -1
            tied = lax.optimization_barrier(tied)
            if k > FLIGHT:
                chunks[steps[k - 1][0]] = tied["before"]
            chunks[j], got[last] = tied["chunk"], tied["got"]
            mate = tied.get("mate", mate)
        if step == 0:
            got[j, 0] = routed(chunks[j], (0, 1))
        elif step == 1:
            got[j, 1] = routed(chunks[j], (1, 0))
        else:
            got[j, 2] = routed(got[j, 0], (1, 0))
        if ready >= 0:
            product(ready, firsts.get(ready - 1, ()))
    for i in range(len(firsts), count):
        if i == count - 1:
            place, seconds = lax.optimization_barrier((place, seconds))
        product(i, firsts[i - 1] if i == 2 else ())
    for i in range(count):
        if i not in seconds:
            keep, send = halve(*firsts[i])
            seconds[i] = keep, swapped(send, 2, "space")
    seconds = {i: finished(*seconds[i]) for i in seconds}
    edge = (seconds[0][0] + seconds[0][1])[0, :WINDOW]
    last, came = seconds[count - 1]
    edge, last = lax.optimization_barrier((edge, last))
    rim = rimmed(edge, core, planes, 2 * chips)
    rim, came = lax.optimization_barrier((rim, came))
    seconds[count - 1] = last, came
    own, swap, near, far = collect(
        [seconds[j][0] for j in range(count)], [seconds[j][1] for j in range(count)]
    )
    size = 2 * chips
    swap = swapped(swap, 1)
    first = lax.ppermute(far, "tm", [(i + 1, i) for i in range(1, size - 1, 2)])
    second = lax.ppermute(near, "tm", [(i + 2, i) for i in range(1, size - 2, 2)])
    return window(scale, core.reshape(1), own, swap, near, first, second, rim)


def solution(mesh):
    placed = (P("space", "tm"),)
    return jax.shard_map(
        local, mesh=mesh, in_specs=placed, out_specs=P("tm", "space"), check_vma=False
    )
```

```python
import functools

import jax
import jax.numpy as jnp
from jax import lax
from jax.experimental import pallas as pl
from jax.experimental.pallas import tpu as pltpu
from jax.sharding import PartitionSpec as P

WINDOW = 16
FLIGHT = 3
PARTS = (3, 3, 3, 2, 1)
DEPTH = 512
MEMORY = 12 * 2**20


def params(factor=1):
    return pltpu.CompilerParams(vmem_limit_bytes=factor * MEMORY)


def swapped(block, bit, axis="tm"):
    size = lax.axis_size(axis)
    return lax.ppermute(block, axis, [(i, i ^ bit) for i in range(size)])


def shifted(block, axis, distance):
    devices = range(lax.axis_size(axis))
    route = [(i - distance, i) for i in devices if i - distance in devices]
    return lax.ppermute(block, axis, route)


def split(value):
    high = value.astype(jnp.bfloat16)
    low = (value - high.astype(jnp.float32)).astype(jnp.bfloat16)
    return high, low


def turn_kernel(source, *chunks):
    turned = source[...].T
    start = 0
    for chunk in chunks:
        chunk[...] = turned[start : start + chunk.shape[0]]
        start += chunk.shape[0]


def turn(source, widths):
    rows, columns = source.shape
    step = 512
    return pl.pallas_call(
        turn_kernel,
        grid=(rows // step,),
        in_specs=[pl.BlockSpec((step, columns), lambda k: (k, 0))],
        out_specs=[pl.BlockSpec((width, step), lambda k: (0, k)) for width in widths],
        out_shape=[jax.ShapeDtypeStruct((width, rows), jnp.float32) for width in widths],
        compiler_params=params(),
    )(source)


def multiply_kernel(steps, count, place, own, mate, *refs):
    pieces, (*earlier, keep, send, total) = refs[:count], refs[count:]
    step = pl.program_id(0)
    left_high, left_low = split(jnp.concatenate([piece[...] for piece in pieces], 0))
    right_high, right_low = split(jnp.concatenate([own[...], mate[...]], 1))
    left = jnp.concatenate([left_high, left_low, left_high], 1)
    right = jnp.concatenate([right_high, right_high, right_low], 0)
    partial = jnp.dot(left, right, preferred_element_type=jnp.float32)

    if earlier:
        kept, came, first, second = earlier

        @pl.when(step == 0)
        def _():
            half = first.shape[0]
            first[...] = kept[:half] + came[:half]
            second[...] = kept[half:] + came[half:]

    @pl.when(step == 0)
    def _():
        total[...] = partial

    @pl.when(jnp.logical_and(step > 0, step < steps - 1))
    def _():
        total[...] += partial

    @pl.when(step == steps - 1)
    def _():
        ready = total[...] + partial
        count, width = keep.shape[:2]
        for offset in range(2 * count):
            block = ready[offset * width : (offset + 1) * width]
            distance = place[offset]
            slot, rest, bit = 0, lax.shift_right_logical(distance, 1), count // 2
            while bit:
                slot = slot + bit * lax.bitwise_and(rest, 1)
                rest, bit = lax.shift_right_logical(rest, 1), bit // 2
            odd = lax.bitwise_and(distance, 1)

            @pl.when(odd == 0)
            def _():
                keep[slot] = block

            @pl.when(odd == 1)
            def _():
                send[slot] = block


def multiply(place, own, mate, pieces, earlier, flops):
    depth, block = own.shape
    steps = depth // DEPTH
    width = pieces[0].shape[0]
    chips = sum(piece.shape[0] for piece in pieces) // width
    shape = (chips // 2, width, 2 * block)
    shapes = [(array.shape[0] // 2,) + array.shape[1:] for array in earlier] + [shape] * 2
    whole = lambda shape: pl.BlockSpec(shape, lambda k: (0, 0, 0))
    right = pl.BlockSpec((DEPTH, block), lambda k: (k, 0))
    return pl.pallas_call(
        functools.partial(multiply_kernel, steps, len(pieces)),
        grid=(steps,),
        in_specs=[pl.BlockSpec(memory_space=pltpu.SMEM), right, right]
        + [pl.BlockSpec((p.shape[0], DEPTH), lambda k: (0, k)) for p in pieces]
        + [whole(array.shape) for array in earlier],
        out_specs=[whole(shape) for shape in shapes],
        out_shape=[jax.ShapeDtypeStruct(shape, jnp.float32) for shape in shapes],
        scratch_shapes=[pltpu.VMEM((chips * width, 2 * block), jnp.float32)],
        compiler_params=params(5),
        cost_estimate=pl.CostEstimate(flops=flops, bytes_accessed=1, transcendentals=0),
    )(place, own, mate, *pieces, *earlier)


def window_kernel(scale, core, own, swap, near, first, second, rim, out, wide):
    rows, columns = out.shape
    block = columns // 2

    @pl.when(core[0] == 0)
    def _():
        wide[:rows, :block] = own[...].T
        wide[:rows, block:columns] = swap[:, :block].T
        wide[rows:, :block] = near[...]
        wide[rows:, block:columns] = swap[:, block:].T[:WINDOW]

    @pl.when(core[0] == 1)
    def _():
        wide[:rows, :block] = swap[:, :block].T
        wide[:rows, block:columns] = own[...].T
        wide[rows:, :block] = first[...]
        wide[rows:, block:columns] = second[...]

    wide[:, columns:] = jnp.concatenate(
        [
            rim[...].T[: rows + WINDOW],
            jnp.zeros((rows + WINDOW, 128 - WINDOW), jnp.float32),
        ],
        1,
    )
    total = wide[...] * scale
    distance = 1
    while distance < WINDOW:
        moved = pltpu.roll(total, total.shape[0] - distance, 0)
        total = total + pltpu.roll(moved, total.shape[1] - distance, 1)
        distance *= 2
    out[...] = total[:rows, :columns]


def window(scale, core, own, *parts):
    columns, rows = own.shape
    return pl.pallas_call(
        functools.partial(window_kernel, scale),
        in_specs=[pl.BlockSpec(memory_space=pltpu.SMEM)]
        + [pl.BlockSpec(memory_space=pltpu.VMEM)] * (1 + len(parts)),
        out_shape=jax.ShapeDtypeStruct((rows, 2 * columns), jnp.float32),
        scratch_shapes=[pltpu.VMEM((rows + WINDOW, 2 * columns + 128), jnp.float32)],
        compiler_params=params(),
    )(core, own, *parts)


def halve_kernel(keep, came, first, second):
    half = first.shape[0]
    first[...] = keep[:half] + came[:half]
    second[...] = keep[half:] + came[half:]


def halve(keep, came):
    half = (keep.shape[0] // 2,) + keep.shape[1:]
    return pl.pallas_call(
        halve_kernel,
        out_shape=[jax.ShapeDtypeStruct(half, jnp.float32)] * 2,
        compiler_params=params(),
    )(keep, came)


def collect_kernel(count, *refs):
    own, swap, near, far = refs[2 * count :]
    block = own.shape[1]
    start = 0
    for keep, came in zip(refs[:count], refs[count : 2 * count]):
        total = keep[0] + came[0]
        rows = pl.ds(start, total.shape[0])
        own[rows, :] = total[:, :block]
        swap[rows, :block] = total[:, block:]
        start += total.shape[0]
    swap[:, block:] = own[:, :128]
    near[...] = swap[:, :128].T[:WINDOW]
    far[...] = own[:, :128].T[:WINDOW]


def collect(keeps, cames):
    columns = sum(keep.shape[1] for keep in keeps)
    block = keeps[0].shape[2] // 2
    shapes = [(columns, block), (columns, block + 128)] + [(WINDOW, columns)] * 2
    return pl.pallas_call(
        functools.partial(collect_kernel, len(keeps)),
        out_shape=[jax.ShapeDtypeStruct(shape, jnp.float32) for shape in shapes],
        compiler_params=params(),
    )(*keeps, *cames)


def moved(value, planes, size, source, target):
    pairs = []
    for chip in range(size // 2):
        start, end = source(chip), target(chip)
        if start < size:
            pairs += [((z + 1) * size + start, z * size + end) for z in range(planes - 1)]
    return lax.ppermute(value, ("space", "tm"), pairs)


def rimmed(edge, core, planes, size):
    block = edge.shape[1] // 2
    zero = moved(edge, planes, size, lambda chip: 2 * chip, lambda chip: 2 * chip)
    one = moved(edge, planes, size, lambda chip: 2 * chip, lambda chip: 2 * chip + 1)
    next_ = moved(
        edge[:, :128], planes, size, lambda chip: 2 * chip + 2, lambda chip: 2 * chip + 1
    )
    return jnp.where(
        core == 0, zero[:, : block + 128], jnp.concatenate([one[:, block:], next_], 1)
    )


def finished(keep, came):
    bit = 2
    while keep.shape[0] > 1:
        bit *= 2
        keep, send = halve(keep, came)
        came = swapped(send, bit, "space")
    return keep, came


def routed(block, ways):
    size = lax.axis_size("tm")
    return lax.ppermute(block, "tm", [(i, i ^ (2 << ways[i % 2])) for i in range(size)])


def local(snapshots):
    tm, space = lax.axis_index("tm"), lax.axis_index("space")
    chips, planes = lax.axis_size("tm") // 2, lax.axis_size("space")
    core = lax.rem(tm, 2)
    depth, block = snapshots.shape
    scale = 1.0 / (depth * planes * WINDOW)
    offsets = [jnp.int32(0), 1 + core, 2 - core, jnp.int32(3)]
    bit = 4
    while bit < chips:
        offsets += [lax.bitwise_xor(offset, bit) for offset in offsets]
        bit *= 2
    place = lax.bitwise_xor(jnp.stack(offsets), lax.bitwise_xor(lax.div(tm, 2), space))

    chunks = list(turn(snapshots, [block * part // sum(PARTS) for part in PARTS]))
    mate = swapped(snapshots, 1)
    count = len(chunks)
    steps = [(0, 0)] + [(j + (step == 0), step) for j in range(count) for step in (1, 0, 2)]
    steps.remove((count, 0))
    got, firsts, seconds = {}, {}, {}

    def product(j, earlier=(), flops=1):
        pieces = [chunks[j]] + [got[j, step] for step in range(3)]
        bit = 4
        while bit < chips:
            pieces += [swapped(piece, 2 * bit) for piece in pieces]
            bit *= 2
        *halved, keep, send = multiply(
            place, snapshots, mate, pieces, earlier, flops
        )
        firsts[j] = keep, swapped(send, 1, "space")
        if halved:
            seconds[j - 1] = halved[0], swapped(halved[1], 2, "space")

    for k, (j, step) in enumerate(steps):
        tied = {"chunk": chunks[j]}
        ready = -1
        if k >= FLIGHT:
            last = steps[k - FLIGHT]
            tied["got"] = got[last]
            if k == FLIGHT:
                tied["mate"] = mate
            if k > FLIGHT:
                tied["before"] = chunks[steps[k - 1][0]]
            ready = k // FLIGHT - 2 if k % FLIGHT == FLIGHT - 1 else -1
            tied = lax.optimization_barrier(tied)
            if k > FLIGHT:
                chunks[steps[k - 1][0]] = tied["before"]
            chunks[j], got[last] = tied["chunk"], tied["got"]
            mate = tied.get("mate", mate)
        if step == 0:
            got[j, 0] = routed(chunks[j], (0, 1))
        elif step == 1:
            got[j, 1] = routed(chunks[j], (1, 0))
        else:
            got[j, 2] = routed(got[j, 0], (1, 0))
        if ready >= 0:
            product(ready, firsts.get(ready - 1, ()))
    for i in range(len(firsts), count):
        if i == count - 1:
            keep, send = halve(*firsts[i - 2])
            came = swapped(send, 2, "space")
            place, seconds[0], keep = lax.optimization_barrier((place, seconds[0], keep))
            seconds[i - 2] = keep, came
        product(i, flops=1 if i == count - 1 else 1)
    for i in range(count):
        if i not in seconds:
            keep, send = halve(*firsts[i])
            seconds[i] = keep, swapped(send, 2, "space")
    seconds = {i: finished(*seconds[i]) for i in seconds}
    edge = (seconds[0][0] + seconds[0][1])[0, :WINDOW]
    last, came = seconds[count - 1]
    edge, last = lax.optimization_barrier((edge, last))
    rim = rimmed(edge, core, planes, 2 * chips)
    rim, came = lax.optimization_barrier((rim, came))
    seconds[count - 1] = last, came
    own, swap, near, far = collect(
        [seconds[j][0] for j in range(count)], [seconds[j][1] for j in range(count)]
    )
    size = 2 * chips
    swap = swapped(swap, 1)
    first = lax.ppermute(far, "tm", [(i + 1, i) for i in range(1, size - 1, 2)])
    second = lax.ppermute(near, "tm", [(i + 2, i) for i in range(1, size - 2, 2)])
    return window(scale, core.reshape(1), own, swap, near, first, second, rim)


def solution(mesh):
    placed = (P("space", "tm"),)
    return jax.shard_map(
        local, mesh=mesh, in_specs=placed, out_specs=P("tm", "space"), check_vma=False
    )
```
